32 devices in a mesh: replica: 2 (over y), tensor: 8 (over z, x), dp: 2 (over core).
Axes of the slice: x: 2, y: 2, z: 4, core: 2. Of those that a mesh axis runs over, the one named last changes fastest.
Arguments:
- queries: bfloat16 [4, 16384], P(('replica', 'dp')), parts along dimension 0, may hold values from -32 to 32
- new_keys: bfloat16 [4, 1024], P(('replica', 'dp')), parts along dimension 0, may hold values from -6 to 6
- new_values: bfloat16 [4, 1024], P(('replica', 'dp')), parts along dimension 0, may hold values from -6 to 6
- key_cache: bfloat16 [4, 256, 1024], P(('replica', 'dp'), 'tensor'), parts along dimension 0, may hold values from -8 to 8
- value_cache: bfloat16 [4, 256, 1024], P(('replica', 'dp'), 'tensor'), parts along dimension 0, may hold values from -6 to 6
- cache_lengths: int32 [4], P(('replica', 'dp')), parts along dimension 0, may hold values from 128 to 256, as said below
- out_weight: bfloat16 [16384, 16384], P('tensor'), may hold values from -0.75 to 0.75
- partial_scales: float32 [4, 128], P(('replica', 'dp')), parts along dimension 0, may hold values from 0.0001 to 0.01
- sum_scales: float32 [4, 128], P(('replica', 'dp')), parts along dimension 0, may hold values from 0.001 to 0.1
Outputs:
- projected: bfloat16 [4, 16384], P(('replica', 'dp')), parts along dimension 0
The draws below stay inside these ranges and needn't reach their ends.
There are 2 independent parts, one for each index of `replica`. The reference program is written for one: setup_inputs(seed, part) draws one part's arguments, and reference() takes and returns one part's arrays. A program takes and returns all parts, laid end to end along the dimension named above; an argument that names none is the same for every part. Nothing has to cross between parts.
Inputs may be any that keep to these rules, and one draw needn't show every extreme that they name: `cache_lengths`: every length is a multiple of 128; in each part one row holds exactly 128 tokens and one exactly 256.
All inputs are finite; a program needn't handle non-finite values.
Results may differ from the reference program's by a relative error of at most 0.02.
Values may be sent and summed in bfloat16 or wider, within the bound.
A program may use at most 192 MiB of HBM per device.

```python
import math
import jax
import jax.numpy as jnp
from jax import lax

D = 16384
HEADS = 128
KVH = 8
HD = 128
QB = 128
PAGE = 128
ROWS = 2
CACHE = 256
N_TENSOR = 8


def draw_queries(key, part):
    own_key = jax.random.fold_in(key, 1)
    return jnp.clip(jax.random.normal(own_key, (ROWS, HEADS * HD), jnp.float32), -6.0, 6.0).astype(jnp.bfloat16)


def draw_key_cache(key, part):
    own_key = jax.random.fold_in(key, 2)
    return jnp.clip(jax.random.normal(own_key, (ROWS, CACHE, KVH * HD), jnp.float32), -6.0, 6.0).astype(jnp.bfloat16)


def draw_cache_lengths(key, part):
    own_key = jax.random.fold_in(key, 3)
    count_key, order_key = jax.random.split(own_key)
    page_total = CACHE // PAGE
    pages_used = jax.random.randint(count_key, (ROWS,), 1, page_total + 1)
    ranking = jax.random.permutation(order_key, ROWS)
    pages_used = jnp.where(ranking == 0, page_total, pages_used)
    pages_used = jnp.where(ranking == 1, 1, pages_used)
    return (pages_used * PAGE).astype(jnp.int32)


def spiked(drawn, stream_key, source, target, shards_of, factor):
    def block_of(dim):
        return (jnp.arange(drawn.shape[dim]) // (drawn.shape[dim] // shards_of)).reshape((-1,) + (1,) * (drawn.ndim - 1 - dim))

    near = jax.random.permutation(stream_key, shards_of)[block_of(target)]
    second = (block_of(target) + shards_of // 2) % shards_of
    return jnp.where((block_of(source) == near) | (block_of(source) == second), factor * drawn, drawn)


def level_of(key, dims, cuts, least, high):
    level, own = 1.0, jax.random.fold_in(key, 6)
    for position, blocks in cuts:
        heights = jnp.exp(jax.random.uniform(jax.random.fold_in(own, position), (blocks,), jnp.float32, least / len(cuts), high / len(cuts)))
        level = level * jnp.repeat(heights, dims[position] // blocks).reshape([-1 if axis == position else 1 for axis in range(len(dims))])
    return level


def normal_values(key, dims, deviation, most, cuts=(), kind=jnp.bfloat16):
    gain = level_of(key, dims, cuts, -0.22, 0.18) if cuts else 1.0
    values = jax.random.normal(key, dims, jnp.float32) * deviation * gain
    return jnp.minimum(jnp.maximum(values, -most), most).astype(kind)


def bell_draw_with(key, shape, width, reach, shards, heavy, held_as=jnp.bfloat16):
    values = width * jax.random.normal(key, shape, jnp.float32)
    if shards:
        values = values * level_of(key, shape, shards, -0.22, 0.18)
    return jnp.clip(spiked(values, jax.random.fold_in(key, 3), *heavy), -reach, reach).astype(held_as)


def setup_inputs(seed: int = 0, part: int = 0) -> dict:
    keys = jax.random.split(jax.random.key(seed), 10)
    part_keys = jax.random.split(jax.random.fold_in(keys[9], part), 10)
    queries = draw_queries(jax.random.fold_in(jax.random.fold_in(keys[9], part), 71), part)
    new_keys = normal_values(part_keys[1], (ROWS, KVH * HD), 1.0, 6.0, ((0, 2),))
    new_values = normal_values(part_keys[2], (ROWS, KVH * HD), 1.0, 6.0, ((0, 2),))
    key_cache = draw_key_cache(jax.random.fold_in(jax.random.fold_in(keys[9], part), 71), part)
    value_cache = normal_values(part_keys[4], (ROWS, CACHE, KVH * HD), 1.0, 6.0, ((0, 2), (1, 8)))
    cache_lengths = draw_cache_lengths(jax.random.fold_in(jax.random.fold_in(keys[9], part), 71), part)
    out_weight = bell_draw_with(keys[6], (HEADS * HD, D), HD ** -0.5, 0.75, ((0, 8),), (0, 1, 8, 2.0))
    partial_scales = jnp.clip(jnp.exp(math.log(0.01) - 4.6051702 * jax.random.uniform(part_keys[7], (ROWS, D // QB), jnp.float32) ** level_of(part_keys[7], (ROWS, D // QB), ((0, 2),), -0.2, 0.2)), 0.0001, 0.01)
    sum_scales = jnp.clip(jnp.exp(math.log(0.1) - 4.6051702 * jax.random.uniform(part_keys[8], (ROWS, D // QB), jnp.float32) ** level_of(part_keys[8], (ROWS, D // QB), ((0, 2),), -0.2, 0.2)), 0.001, 0.1)
    return dict(queries=queries, new_keys=new_keys, new_values=new_values, key_cache=key_cache, value_cache=value_cache, cache_lengths=cache_lengths, out_weight=out_weight, partial_scales=partial_scales, sum_scales=sum_scales)


def reference(queries, new_keys, new_values, key_cache, value_cache, cache_lengths, out_weight, partial_scales, sum_scales):
    row_count = queries.shape[0]
    group_size = HEADS // KVH
    inv_root = 1.0 / math.sqrt(HD)
    queried = queries.astype(jnp.float32).reshape(row_count, KVH, group_size, HD)
    keys_all = key_cache.astype(jnp.float32).reshape(row_count, CACHE, KVH, HD)
    values_all = value_cache.astype(jnp.float32).reshape(row_count, CACHE, KVH, HD)
    scores = jnp.einsum('rkgd,rckd->rkgc', queried, keys_all) * inv_root
    fresh_score = jnp.einsum('rkgd,rkd->rkg', queried, new_keys.astype(jnp.float32).reshape(row_count, KVH, HD)) * inv_root
    positions = jnp.arange(CACHE, dtype=jnp.int32)
    live_mask = (positions[None, :] < cache_lengths.astype(jnp.int32)[:, None])[:, None, None, :]
    masked = jnp.where(live_mask, scores, -1e+30)
    best_score = jnp.maximum(lax.optimization_barrier(jnp.max(masked, axis=-1)), fresh_score)
    weights = jnp.where(live_mask, jnp.exp(masked - best_score[..., None]), 0.0).astype(jnp.bfloat16)
    weights_wide = weights.astype(jnp.float32)
    new_factor = jnp.exp(fresh_score - best_score)
    total_mass = lax.optimization_barrier(jnp.sum(weights_wide, axis=-1)) + new_factor
    fresh_value = new_values.astype(jnp.float32).reshape(row_count, KVH, 1, HD)
    numer_sum = jnp.einsum('rkgc,rckd->rkgd', weights_wide, values_all) + new_factor[..., None] * fresh_value
    attended = (numer_sum / total_mass[..., None]).reshape(row_count, HEADS * HD).astype(jnp.bfloat16)
    heads_here = HEADS // N_TENSOR
    group_width = heads_here * HD
    block_count = D // QB
    pieces = attended.reshape(row_count, N_TENSOR, group_width).transpose(1, 0, 2)
    weight_blocks = out_weight.reshape(N_TENSOR, group_width, D)

    def accumulate(running, inputs):
        partial_value = jnp.dot(inputs[0], inputs[1], preferred_element_type=jnp.float32)
        coded_terms = jnp.clip(partial_value.reshape(row_count, block_count, QB) / partial_scales[..., None], -448.0, 448.0).astype(jnp.bfloat16)
        coded_terms = lax.optimization_barrier(coded_terms)
        return (running + coded_terms.astype(jnp.float32), None)
    summed, _ = lax.scan(accumulate, jnp.zeros((row_count, block_count, QB), jnp.float32), (pieces, weight_blocks))
    reduced = summed * partial_scales[..., None]
    recoded = jnp.clip(reduced / sum_scales[..., None], -448.0, 448.0).astype(jnp.bfloat16)
    recoded = lax.optimization_barrier(recoded)
    return (recoded.astype(jnp.float32) * sum_scales[..., None]).reshape(row_count, D).astype(jnp.bfloat16)
```

```python
import math

import jax
import jax.numpy as jnp
from jax import lax
from jax.experimental import pallas as pl
from jax.experimental.pallas import tpu as pltpu
from jax.sharding import PartitionSpec as P

D = 16384
HEADS = 128
KVH = 8
HD = 128
QB = 128


def shards(
    queries,
    new_keys,
    new_values,
    key_cache,
    value_cache,
    cache_lengths,
    out_weight,
    partial_scales,
    sum_scales,
):
    shard_index = lax.axis_index("tensor")
    shard_count = lax.axis_size("tensor")
    row_count = queries.shape[0]
    window = key_cache.shape[1]
    group_size = HEADS // KVH
    heads_here = HEADS // shard_count
    inv_root = 1.0 / math.sqrt(HD)
    query_heads = queries.reshape(row_count, KVH, group_size, HD)
    keys_local = key_cache.reshape(row_count, window, KVH, HD)
    values_local = value_cache.reshape(row_count, window, KVH, HD)
    scores = (
        jnp.einsum("rkgd,rckd->rkgc", query_heads, keys_local, preferred_element_type=jnp.float32)
        * inv_root
    )
    positions = shard_index * window + jnp.arange(window, dtype=jnp.int32)
    live_mask = (positions[None, :] < cache_lengths[:, None])[:, None, None, :]
    masked = jnp.where(live_mask, scores, -1e30)
    local_top = jnp.max(masked, axis=-1)
    weights = jnp.where(live_mask, jnp.exp(masked - local_top[..., None]), 0.0).astype(jnp.bfloat16)
    local_mass = jnp.sum(weights.astype(jnp.float32), axis=-1)
    local_numer = jnp.einsum(
        "rkgc,rckd->rkgd", weights, values_local, preferred_element_type=jnp.float32
    )
    top_parts = local_top.reshape(row_count, HEADS)
    mass_parts = local_mass.reshape(row_count, HEADS)
    numer_parts = local_numer.reshape(row_count, HEADS, HD)
    first_head = shard_index * heads_here
    start_state = (
        jnp.full((row_count, heads_here), -1e30, jnp.float32),
        jnp.zeros((row_count, heads_here), jnp.float32),
        jnp.zeros((row_count, heads_here, HD), jnp.float32),
    )
    piece_top = lax.dynamic_slice_in_dim(
        lax.all_gather(top_parts[None].astype(jnp.bfloat16), "tensor", axis=0, tiled=True).astype(
            jnp.float32
        ),
        first_head,
        heads_here,
        2,
    )
    piece_mass = lax.dynamic_slice_in_dim(
        lax.all_gather(mass_parts[None].astype(jnp.bfloat16), "tensor", axis=0, tiled=True).astype(
            jnp.float32
        ),
        first_head,
        heads_here,
        2,
    )
    piece_numer = lax.dynamic_slice_in_dim(
        lax.all_gather(numer_parts[None].astype(jnp.bfloat16), "tensor", axis=0, tiled=True).astype(
            jnp.float32
        ),
        first_head,
        heads_here,
        2,
    )
    joined_top = jnp.maximum(start_state[0], jnp.max(piece_top, axis=0))
    piece_factor = jnp.exp(piece_top - joined_top)
    carry_factor = jnp.exp(start_state[0] - joined_top)
    joined_mass = start_state[1] * carry_factor + jnp.sum(piece_mass * piece_factor, axis=0)
    joined_numer = start_state[2] * carry_factor[..., None] + jnp.sum(
        piece_numer * piece_factor[..., None], axis=0
    )
    own_query = lax.dynamic_slice_in_dim(queries, first_head * HD, heads_here * HD, 1).reshape(
        row_count, heads_here, HD
    )
    kv_index = (first_head + jnp.arange(heads_here, dtype=jnp.int32)) // group_size
    picker = (kv_index[:, None] == jnp.arange(KVH, dtype=jnp.int32)[None, :]).astype(jnp.float32)
    own_key = jnp.einsum(
        "hk,rkd->rhd",
        picker,
        new_keys.reshape(row_count, KVH, HD).astype(jnp.float32),
        precision=lax.Precision.HIGHEST,
    )
    own_value = jnp.einsum(
        "hk,rkd->rhd",
        picker,
        new_values.reshape(row_count, KVH, HD).astype(jnp.float32),
        precision=lax.Precision.HIGHEST,
    )
    fresh_score = jnp.sum(own_query.astype(jnp.float32) * own_key, axis=-1) * inv_root
    best_score = jnp.maximum(joined_top, fresh_score)
    old_factor = jnp.exp(joined_top - best_score)
    new_factor = jnp.exp(fresh_score - best_score)
    attended = (joined_numer * old_factor[..., None] + new_factor[..., None] * own_value) / (
        joined_mass * old_factor + new_factor
    )[..., None]
    attended = attended.astype(jnp.bfloat16).reshape(row_count, heads_here * HD)
    partial_value = jnp.dot(attended, out_weight, preferred_element_type=jnp.float32)
    block_count = D // QB
    coded_narrow = jnp.clip(
        partial_value.reshape(row_count, block_count, QB) / partial_scales[..., None], -448.0, 448.0
    ).astype(jnp.bfloat16)
    coded_narrow = lax.optimization_barrier(coded_narrow).reshape(row_count, D)
    summed = lax.psum(coded_narrow.astype(jnp.float32), "tensor")
    reduced = summed.reshape(row_count, block_count, QB) * partial_scales[..., None]
    recoded = jnp.clip(reduced / sum_scales[..., None], -448.0, 448.0).astype(jnp.bfloat16)
    gathered = recoded.reshape(row_count, D)
    result = (
        gathered.reshape(row_count, block_count, QB).astype(jnp.float32) * sum_scales[..., None]
    )
    return result.reshape(row_count, D).astype(jnp.bfloat16)


MESH = pl.DeviceIdType.MESH
QUAD = 4
GROUP = HEADS // KVH
CHUNKS = KVH
CHUNK = D // CHUNKS // QUAD
BLOCKS = CHUNK // QB


def device(row, shard):
    return {"replica": row // 2, "tensor": shard, "dp": row % 2}


def flipped(shard, k):
    total = 0
    for bit in (1, 2, 4):
        a = (shard // bit) % 2
        b = (k // bit) % 2
        total = total + bit * (a + b - 2 * a * b)
    return total


def kernel(
    q_hbm, nk_hbm, nv_hbm, k_hbm, v_hbm, len_hbm, w_hbm, ps_hbm, ss_hbm,
    out_ref,
    q_raw, nk, nv, keys, values, lens, first, second, wbuf, q_rows,
    snd1, rcv1, att, snd2, rcv2, scales, fin, gath,
    in_sem, w_sem, s1, r1, s2, r2, s3, r3, s4, r4,
):
    rep, me, dp = lax.axis_index("replica"), lax.axis_index("tensor"), lax.axis_index("dp")
    row = rep * 2 + dp
    window = keys.shape[0]
    inv_root = 1.0 / math.sqrt(HD)

    small = [
        pltpu.make_async_copy(a, b, in_sem.at[i])
        for i, (a, b) in enumerate(
            [
                (q_hbm, q_raw), (k_hbm.at[0], keys), (len_hbm, lens), (v_hbm.at[0], values),
                (nk_hbm, nk), (nv_hbm, nv), (ps_hbm, first), (ss_hbm, second),
            ]
        )
    ]
    for copy in small:
        copy.start()

    def weight_copy(i):
        shard = flipped(me, CHUNKS - 1 - i)
        start = pl.multiple_of(shard * (QUAD * CHUNK) + row * CHUNK, CHUNK)
        return pltpu.make_async_copy(w_hbm.at[:, pl.ds(start, CHUNK)], wbuf.at[i], w_sem.at[i])

    for i in range(CHUNKS):
        weight_copy(i).start()

    barrier = pltpu.get_barrier_semaphore()
    total_devices = QUAD * CHUNKS
    place = row * CHUNKS + me

    def greet(j, carry):
        other = (place + j) % total_devices
        pl.semaphore_signal(
            barrier, inc=1, device_id=device(other // CHUNKS, other % CHUNKS), device_id_type=MESH
        )
        return carry

    lax.fori_loop(1, total_devices, greet, 0)

    for copy in small:
        copy.wait()

    for h in range(HEADS):
        q_rows[h : h + 1, :] = q_raw[0:1, h * HD : (h + 1) * HD].astype(jnp.float32)

    length = lens[0]
    live = (me * window + lax.broadcasted_iota(jnp.int32, (GROUP, window), 1)) < length
    lane = lax.broadcasted_iota(jnp.int32, (GROUP, HD), 1)
    for k in range(KVH):
        query = q_rows[k * GROUP : (k + 1) * GROUP, :].astype(jnp.bfloat16)
        score = (
            lax.dot_general(
                query, keys[:, k * HD : (k + 1) * HD], (((1,), (1,)), ((), ())),
                preferred_element_type=jnp.float32,
            )
            * inv_root
        )
        score = jnp.where(live, score, -1e30)
        top = jnp.max(score, axis=-1, keepdims=True).astype(jnp.bfloat16).astype(jnp.float32)
        weight = jnp.where(live, jnp.exp(score - top), 0.0).astype(jnp.bfloat16)
        mass = jnp.sum(weight.astype(jnp.float32), axis=-1, keepdims=True)
        numer = jnp.dot(weight, values[:, k * HD : (k + 1) * HD], preferred_element_type=jnp.float32)
        coarse = mass.astype(jnp.bfloat16).astype(jnp.float32)
        stats = jnp.where(lane == 0, top, jnp.where(lane == 1, coarse, mass - coarse))
        snd1[k, 0:GROUP, :] = numer.astype(jnp.bfloat16)
        snd1[k, GROUP : 2 * GROUP, :] = stats.astype(jnp.bfloat16)

    for i in range(4 * BLOCKS):
        scales[0, i // BLOCKS, i % BLOCKS, :] = jnp.full((QB,), first[0, me * (QUAD * BLOCKS) + i], jnp.float32)
        scales[1, i // BLOCKS, i % BLOCKS, :] = jnp.full((QB,), second[0, me * (QUAD * BLOCKS) + i], jnp.float32)

    pl.semaphore_wait(barrier, total_devices - 1)

    for k in range(CHUNKS - 1, 0, -1):
        shard = flipped(me, k)
        pltpu.make_async_remote_copy(
            snd1.at[shard], rcv1.at[me], s1, r1, device_id=device(row, shard), device_id_type=MESH
        ).start()
    rcv1[me] = snd1[me]
    own_query = q_rows[pl.ds(pl.multiple_of(me * GROUP, GROUP), GROUP), :]
    own = pl.ds(pl.multiple_of(me * HD, HD), HD)
    own_key = nk[:, own].astype(jnp.float32)
    own_value = nv[:, own].astype(jnp.float32)
    fresh = jnp.sum(own_query * own_key, axis=-1, keepdims=True) * inv_root
    pltpu.make_async_copy(rcv1.at[pl.ds(0, CHUNKS - 1)], rcv1.at[pl.ds(0, CHUNKS - 1)], r1).wait()

    got = [rcv1[t].astype(jnp.float32) for t in range(CHUNKS)]
    tops = [g[GROUP:, 0:1] for g in got]
    best = fresh
    for top in tops:
        best = jnp.maximum(best, top)
    fresh_factor = jnp.exp(fresh - best)
    mass = fresh_factor
    numer = fresh_factor * own_value
    for g, top in zip(got, tops):
        factor = jnp.exp(top - best)
        mass = mass + factor * (g[GROUP:, 1:2] + g[GROUP:, 2:3])
        numer = numer + factor * g[:GROUP]
    mine = pl.ds(pl.multiple_of(row * GROUP, GROUP), GROUP)
    att[mine, :] = (numer / mass).astype(jnp.bfloat16).astype(jnp.float32)

    for j in range(1, QUAD):
        pltpu.make_async_remote_copy(
            att.at[mine], att.at[mine], s2, r2,
            device_id=device((row + j) % QUAD, me), device_id_type=MESH,
        ).start()
    pltpu.make_async_copy(att.at[pl.ds(0, 3 * GROUP)], att.at[pl.ds(0, 3 * GROUP)], r2).wait()
    x = jnp.concatenate(
        [att[pl.ds(h, QUAD, stride=GROUP), :] for h in range(GROUP)], axis=1
    ).astype(jnp.bfloat16)

    def product(i):
        weight_copy(i).wait()
        y = jnp.dot(x, wbuf[i], preferred_element_type=jnp.float32)
        for r in range(QUAD):
            for b in range(BLOCKS):
                snd2[i * QUAD + r, b : b + 1, :] = y[r : r + 1, b * QB : (b + 1) * QB]

    def send(i, r, shard):
        pltpu.make_async_remote_copy(
            snd2.at[i * QUAD + r], rcv2.at[me * QUAD + row], s3, r3,
            device_id=device(r, shard), device_id_type=MESH,
        ).start()

    def step(i, carry):
        product(i)
        shard = flipped(me, CHUNKS - 1 - i)
        for r in range(QUAD):
            send(i, r, shard)
        return carry

    lax.fori_loop(0, CHUNKS - 1, step, 0)
    product(CHUNKS - 1)
    for j in range(1, QUAD):
        send(CHUNKS - 1, (row + j) % QUAD, me)
    rcv2[me * QUAD + row] = snd2[(CHUNKS - 1) * QUAD + row]
    every = pl.ds(0, total_devices - 1)
    pltpu.make_async_copy(rcv2.at[every], rcv2.at[every], r3).wait()

    for q in range(QUAD):
        first_scale, second_scale = scales[0, q], scales[1, q]
        total = jnp.zeros((BLOCKS, QB), jnp.float32)
        for t in range(CHUNKS):
            coded = jnp.clip(rcv2[t * QUAD + q] / first_scale, -448.0, 448.0)
            total = total + coded.astype(jnp.bfloat16).astype(jnp.float32)
        recoded = jnp.clip(total * first_scale / second_scale, -448.0, 448.0).astype(jnp.bfloat16)
        fin[q * BLOCKS : (q + 1) * BLOCKS, :] = recoded.astype(jnp.float32) * second_scale
    own_rows = pl.ds(pl.multiple_of(me * QUAD * BLOCKS, QUAD * BLOCKS), QUAD * BLOCKS)
    gath[own_rows, :] = fin[...].astype(jnp.bfloat16)

    for k in range(CHUNKS - 1, 0, -1):
        pltpu.make_async_remote_copy(
            gath.at[own_rows], gath.at[own_rows], s4, r4,
            device_id=device(row, flipped(me, k)), device_id_type=MESH,
        ).start()
    pltpu.make_async_copy(snd1.at[pl.ds(0, CHUNKS - 1)], snd1.at[pl.ds(0, CHUNKS - 1)], s1).wait()
    pltpu.make_async_copy(att.at[pl.ds(0, 3 * GROUP)], att.at[pl.ds(0, 3 * GROUP)], s2).wait()
    pltpu.make_async_copy(snd2.at[every], snd2.at[every], s3).wait()
    most = pl.ds(0, (CHUNKS - 1) * QUAD * BLOCKS)
    pltpu.make_async_copy(gath.at[most], gath.at[most], r4).wait()
    out_ref[...] = gath[...]
    pltpu.make_async_copy(gath.at[most], gath.at[most], s4).wait()


def fused(*arrays):
    window = arrays[3].shape[1]
    depth = arrays[6].shape[0]
    bf16, f32 = jnp.bfloat16, jnp.float32
    dma = pltpu.SemaphoreType.DMA
    out = pl.pallas_call(
        kernel,
        out_shape=jax.ShapeDtypeStruct((D // QB, QB), bf16),
        in_specs=[pl.BlockSpec(memory_space=pl.ANY)] * 9,
        out_specs=pl.BlockSpec(memory_space=pltpu.VMEM),
        scratch_shapes=[
            pltpu.VMEM((1, HEADS * HD), bf16),
            pltpu.VMEM((1, KVH * HD), bf16),
            pltpu.VMEM((1, KVH * HD), bf16),
            pltpu.VMEM((window, KVH * HD), bf16),
            pltpu.VMEM((window, KVH * HD), bf16),
            pltpu.SMEM((1,), jnp.int32),
            pltpu.SMEM((1, D // QB), f32),
            pltpu.SMEM((1, D // QB), f32),
            pltpu.VMEM((CHUNKS, depth, CHUNK), bf16),
            pltpu.VMEM((HEADS, HD), f32),
            pltpu.VMEM((CHUNKS, 2 * GROUP, HD), bf16),
            pltpu.VMEM((CHUNKS, 2 * GROUP, HD), bf16),
            pltpu.VMEM((QUAD * GROUP, HD), f32),
            pltpu.VMEM((CHUNKS * QUAD, BLOCKS, QB), f32),
            pltpu.VMEM((CHUNKS * QUAD, BLOCKS, QB), f32),
            pltpu.VMEM((2, QUAD, BLOCKS, QB), f32),
            pltpu.VMEM((QUAD * BLOCKS, QB), f32),
            pltpu.VMEM((D // QB, QB), bf16),
            dma((8,)), dma((CHUNKS,)),
            dma, dma, dma, dma, dma, dma, dma, dma,
        ],
        compiler_params=pltpu.CompilerParams(
            collective_id=0, has_side_effects=True, vmem_limit_bytes=48 * 1024 * 1024
        ),
    )(*arrays)
    return out.reshape(1, D)


def body_for(mesh):
    sizes = dict(mesh.shape)
    if sizes["tensor"] == KVH and sizes["replica"] == 2 and sizes["dp"] == 2:
        return fused
    return shards


def solution(mesh):
    return jax.shard_map(
        body_for(mesh),
        mesh=mesh,
        in_specs=(
            P(("replica", "dp"), None),
            P(("replica", "dp"), None),
            P(("replica", "dp"), None),
            P(("replica", "dp"), "tensor", None),
            P(("replica", "dp"), "tensor", None),
            P(("replica", "dp")),
            P("tensor", None),
            P(("replica", "dp"), None),
            P(("replica", "dp"), None),
        ),
        out_specs=P(("replica", "dp"), None),
        check_vma=False,
    )
```

```python
import math

import jax
import jax.numpy as jnp
from jax import lax
from jax.experimental import pallas as pl
from jax.experimental.pallas import tpu as pltpu
from jax.sharding import PartitionSpec as P

D = 16384
HEADS = 128
KVH = 8
HD = 128
QB = 128


def shards(
    queries,
    new_keys,
    new_values,
    key_cache,
    value_cache,
    cache_lengths,
    out_weight,
    partial_scales,
    sum_scales,
):
    shard_index = lax.axis_index("tensor")
    shard_count = lax.axis_size("tensor")
    row_count = queries.shape[0]
    window = key_cache.shape[1]
    group_size = HEADS // KVH
    heads_here = HEADS // shard_count
    inv_root = 1.0 / math.sqrt(HD)
    query_heads = queries.reshape(row_count, KVH, group_size, HD)
    keys_local = key_cache.reshape(row_count, window, KVH, HD)
    values_local = value_cache.reshape(row_count, window, KVH, HD)
    scores = (
        jnp.einsum("rkgd,rckd->rkgc", query_heads, keys_local, preferred_element_type=jnp.float32)
        * inv_root
    )
    positions = shard_index * window + jnp.arange(window, dtype=jnp.int32)
    live_mask = (positions[None, :] < cache_lengths[:, None])[:, None, None, :]
    masked = jnp.where(live_mask, scores, -1e30)
    local_top = jnp.max(masked, axis=-1)
    weights = jnp.where(live_mask, jnp.exp(masked - local_top[..., None]), 0.0).astype(jnp.bfloat16)
    local_mass = jnp.sum(weights.astype(jnp.float32), axis=-1)
    local_numer = jnp.einsum(
        "rkgc,rckd->rkgd", weights, values_local, preferred_element_type=jnp.float32
    )
    top_parts = local_top.reshape(row_count, HEADS)
    mass_parts = local_mass.reshape(row_count, HEADS)
    numer_parts = local_numer.reshape(row_count, HEADS, HD)
    first_head = shard_index * heads_here
    start_state = (
        jnp.full((row_count, heads_here), -1e30, jnp.float32),
        jnp.zeros((row_count, heads_here), jnp.float32),
        jnp.zeros((row_count, heads_here, HD), jnp.float32),
    )
    piece_top = lax.dynamic_slice_in_dim(
        lax.all_gather(top_parts[None].astype(jnp.bfloat16), "tensor", axis=0, tiled=True).astype(
            jnp.float32
        ),
        first_head,
        heads_here,
        2,
    )
    piece_mass = lax.dynamic_slice_in_dim(
        lax.all_gather(mass_parts[None].astype(jnp.bfloat16), "tensor", axis=0, tiled=True).astype(
            jnp.float32
        ),
        first_head,
        heads_here,
        2,
    )
    piece_numer = lax.dynamic_slice_in_dim(
        lax.all_gather(numer_parts[None].astype(jnp.bfloat16), "tensor", axis=0, tiled=True).astype(
            jnp.float32
        ),
        first_head,
        heads_here,
        2,
    )
    joined_top = jnp.maximum(start_state[0], jnp.max(piece_top, axis=0))
    piece_factor = jnp.exp(piece_top - joined_top)
    carry_factor = jnp.exp(start_state[0] - joined_top)
    joined_mass = start_state[1] * carry_factor + jnp.sum(piece_mass * piece_factor, axis=0)
    joined_numer = start_state[2] * carry_factor[..., None] + jnp.sum(
        piece_numer * piece_factor[..., None], axis=0
    )
    own_query = lax.dynamic_slice_in_dim(queries, first_head * HD, heads_here * HD, 1).reshape(
        row_count, heads_here, HD
    )
    kv_index = (first_head + jnp.arange(heads_here, dtype=jnp.int32)) // group_size
    picker = (kv_index[:, None] == jnp.arange(KVH, dtype=jnp.int32)[None, :]).astype(jnp.float32)
    own_key = jnp.einsum(
        "hk,rkd->rhd",
        picker,
        new_keys.reshape(row_count, KVH, HD).astype(jnp.float32),
        precision=lax.Precision.HIGHEST,
    )
    own_value = jnp.einsum(
        "hk,rkd->rhd",
        picker,
        new_values.reshape(row_count, KVH, HD).astype(jnp.float32),
        precision=lax.Precision.HIGHEST,
    )
    fresh_score = jnp.sum(own_query.astype(jnp.float32) * own_key, axis=-1) * inv_root
    best_score = jnp.maximum(joined_top, fresh_score)
    old_factor = jnp.exp(joined_top - best_score)
    new_factor = jnp.exp(fresh_score - best_score)
    attended = (joined_numer * old_factor[..., None] + new_factor[..., None] * own_value) / (
        joined_mass * old_factor + new_factor
    )[..., None]
    attended = attended.astype(jnp.bfloat16).reshape(row_count, heads_here * HD)
    partial_value = jnp.dot(attended, out_weight, preferred_element_type=jnp.float32)
    block_count = D // QB
    coded_narrow = jnp.clip(
        partial_value.reshape(row_count, block_count, QB) / partial_scales[..., None], -448.0, 448.0
    ).astype(jnp.bfloat16)
    coded_narrow = lax.optimization_barrier(coded_narrow).reshape(row_count, D)
    summed = lax.psum(coded_narrow.astype(jnp.float32), "tensor")
    reduced = summed.reshape(row_count, block_count, QB) * partial_scales[..., None]
    recoded = jnp.clip(reduced / sum_scales[..., None], -448.0, 448.0).astype(jnp.bfloat16)
    gathered = recoded.reshape(row_count, D)
    result = (
        gathered.reshape(row_count, block_count, QB).astype(jnp.float32) * sum_scales[..., None]
    )
    return result.reshape(row_count, D).astype(jnp.bfloat16)


MESH = pl.DeviceIdType.MESH
PAIR = 2
GROUP = HEADS // KVH
SHARDS = KVH
PLANES = 4
HALF = D // PLANES // PAIR
PIECES = 2
PIECE = HALF // PIECES
BLOCKS = HALF // QB


def flipped(index, k):
    total = 0
    for bit in (1, 2, 4):
        a = (index // bit) % 2
        b = (k // bit) % 2
        total = total + bit * (a + b - 2 * a * b)
    return total


def kernel(
    q_hbm, nk_hbm, nv_hbm, k_hbm, v_hbm, len_hbm, w_hbm, ps_hbm, ss_hbm,
    out_ref,
    q_raw, nk, nv, keys, values, lens, first, second, wbuf, q_rows,
    snd1, rcv1, att, stage, snd2, rcv2, scales, gath,
    in_sem, w_sem, s1, r1, s2, r2, s3, r3, s4, r4,
):
    rep, me, dp = lax.axis_index("replica"), lax.axis_index("tensor"), lax.axis_index("dp")
    plane, side = me // 2, me % 2
    window = keys.shape[0]
    inv_root = 1.0 / math.sqrt(HD)

    def device(shard, core):
        return {"replica": rep, "tensor": shard, "dp": core}

    small = [
        pltpu.make_async_copy(a, b, in_sem.at[i])
        for i, (a, b) in enumerate(
            [
                (q_hbm, q_raw), (k_hbm.at[0], keys), (len_hbm, lens), (v_hbm.at[0], values),
                (nk_hbm, nk), (nv_hbm, nv), (ps_hbm, first), (ss_hbm, second),
            ]
        )
    ]

    def weight_copy(i, p):
        target = flipped(plane, PLANES - 1 - i)
        start = pl.multiple_of(target * (PAIR * HALF) + dp * HALF + p * PIECE, PIECE)
        slot = i * PIECES + p
        return pltpu.make_async_copy(w_hbm.at[:, pl.ds(start, PIECE)], wbuf.at[slot], w_sem.at[slot])

    barrier = pltpu.get_barrier_semaphore()
    for k in range(SHARDS - 1, -1, -1):
        for c in range(PAIR):
            if k or c:
                pl.semaphore_signal(
                    barrier, inc=1, device_id=device(flipped(me, k), (dp + c) % 2), device_id_type=MESH
                )
    for copy in small:
        copy.start()
    for n in range(0, 4):
        weight_copy(n // PIECES, n % PIECES).start()
    for copy in small:
        copy.wait()

    for h in range(HEADS):
        q_rows[h : h + 1, :] = q_raw[0:1, h * HD : (h + 1) * HD].astype(jnp.float32)

    length = lens[0]
    live = (me * window + lax.broadcasted_iota(jnp.int32, (GROUP, window), 1)) < length
    lane = lax.broadcasted_iota(jnp.int32, (GROUP, HD), 1)
    for k in range(KVH):
        query = q_rows[k * GROUP : (k + 1) * GROUP, :].astype(jnp.bfloat16)
        score = (
            lax.dot_general(
                query, keys[:, k * HD : (k + 1) * HD], (((1,), (1,)), ((), ())),
                preferred_element_type=jnp.float32,
            )
            * inv_root
        )
        score = jnp.where(live, score, -1e30)
        top = jnp.max(score, axis=-1, keepdims=True).astype(jnp.bfloat16).astype(jnp.float32)
        weight = jnp.where(live, jnp.exp(score - top), 0.0).astype(jnp.bfloat16)
        mass = jnp.sum(weight.astype(jnp.float32), axis=-1, keepdims=True)
        numer = jnp.dot(weight, values[:, k * HD : (k + 1) * HD], preferred_element_type=jnp.float32)
        coarse = mass.astype(jnp.bfloat16).astype(jnp.float32)
        stats = jnp.where(lane == 0, top, jnp.where(lane == 1, coarse, mass - coarse))
        snd1[k, 0:GROUP, :] = numer.astype(jnp.bfloat16)
        snd1[k, GROUP : 2 * GROUP, :] = stats.astype(jnp.bfloat16)

    for i in range(PAIR * BLOCKS):
        at = plane * (PAIR * BLOCKS) + i
        scales[0, i : i + 1, :] = jnp.full((1, QB), first[0, at], jnp.float32)
        scales[1, i : i + 1, :] = jnp.full((1, QB), second[0, at], jnp.float32)
    own_query = q_rows[pl.ds(pl.multiple_of(me * GROUP, GROUP), GROUP), :]
    own = pl.ds(pl.multiple_of(me * HD, HD), HD)
    own_key = nk[:, own].astype(jnp.float32)
    own_value = nv[:, own].astype(jnp.float32)
    fresh = jnp.sum(own_query * own_key, axis=-1, keepdims=True) * inv_root

    pl.semaphore_wait(barrier, SHARDS * PAIR - 1)

    for k in range(SHARDS - 1, 0, -1):
        shard = flipped(me, k)
        pltpu.make_async_remote_copy(
            snd1.at[shard], rcv1.at[me], s1, r1, device_id=device(shard, dp), device_id_type=MESH
        ).start()
    for n in range(4, 8):
        weight_copy(n // PIECES, n % PIECES).start()
    rcv1[me] = snd1[me]
    pltpu.make_async_copy(rcv1.at[pl.ds(0, SHARDS - 1)], rcv1.at[pl.ds(0, SHARDS - 1)], r1).wait()

    got = [rcv1[t].astype(jnp.float32) for t in range(SHARDS)]
    tops = [g[GROUP:, 0:1] for g in got]
    best = fresh
    for top in tops:
        best = jnp.maximum(best, top)
    fresh_factor = jnp.exp(fresh - best)
    mass = fresh_factor
    numer = fresh_factor * own_value
    for g, top in zip(got, tops):
        factor = jnp.exp(top - best)
        mass = mass + factor * (g[GROUP:, 1:2] + g[GROUP:, 2:3])
        numer = numer + factor * g[:GROUP]
    mine = pl.ds(pl.multiple_of(dp * GROUP, GROUP), GROUP)
    att[mine, :] = (numer / mass).astype(jnp.bfloat16).astype(jnp.float32)

    swap = pltpu.make_async_remote_copy(
        att.at[mine], att.at[mine], s2, r2, device_id=device(me, 1 - dp), device_id_type=MESH
    )
    swap.start()
    swap.wait_recv()
    x = jnp.concatenate(
        [att[pl.ds(h, PAIR, stride=GROUP), :] for h in range(GROUP)], axis=1
    ).astype(jnp.bfloat16)

    def product(i):
        for p in range(PIECES):
            weight_copy(i, p).wait()
            y = jnp.dot(x, wbuf[i * PIECES + p], preferred_element_type=jnp.float32)
            for b in range(PIECE // QB):
                at = p * (PIECE // QB) + b
                for r in range(PAIR):
                    stage[r, at : at + 1, :] = y[r : r + 1, b * QB : (b + 1) * QB]
        for r in range(PAIR):
            snd2[i * PAIR + r] = stage[r].astype(jnp.bfloat16)

    slot = me * PAIR + dp

    def send(i, r, shard):
        pltpu.make_async_remote_copy(
            snd2.at[i * PAIR + r], rcv2.at[slot], s3, r3,
            device_id=device(shard, r), device_id_type=MESH,
        ).start()

    def step(i, carry):
        product(i)
        target = flipped(plane, PLANES - 1 - i)
        for r in range(PAIR):
            send(i, r, target * 2 + 1 - side)
            send(i, r, target * 2 + side)
        return carry

    lax.fori_loop(0, PLANES - 1, step, 0)
    last = PLANES - 1
    product(last)
    send(last, 0, plane * 2 + 1 - side)
    send(last, 1, plane * 2 + 1 - side)
    send(last, 1 - dp, me)
    rcv2[slot] = snd2[last * PAIR + dp]
    others = pl.ds(0, SHARDS * PAIR - 1)
    pltpu.make_async_copy(rcv2.at[others], rcv2.at[others], r3).wait()

    rows = PAIR * BLOCKS
    for h in range(PAIR):
        part = slice(h * BLOCKS, (h + 1) * BLOCKS)
        first_scale, second_scale = scales[0, part, :], scales[1, part, :]
        total = jnp.zeros((BLOCKS, QB), jnp.float32)
        for t in range(SHARDS):
            coded = jnp.clip(rcv2[t * PAIR + h].astype(jnp.float32) / first_scale, -448.0, 448.0)
            total = total + coded.astype(jnp.bfloat16).astype(jnp.float32)
        recoded = jnp.clip(total * first_scale / second_scale, -448.0, 448.0).astype(jnp.bfloat16)
        at = pl.ds(pl.multiple_of(plane * rows + h * BLOCKS, BLOCKS), BLOCKS)
        gath[at, :] = (recoded.astype(jnp.float32) * second_scale).astype(jnp.bfloat16)

    own_rows = pl.ds(pl.multiple_of(plane * rows, rows), rows)
    for k in range(PLANES - 1, 0, -1):
        pltpu.make_async_remote_copy(
            gath.at[own_rows], gath.at[own_rows], s4, r4,
            device_id=device(flipped(plane, k) * 2 + side, dp), device_id_type=MESH,
        ).start()
    pltpu.make_async_copy(snd1.at[pl.ds(0, SHARDS - 1)], snd1.at[pl.ds(0, SHARDS - 1)], s1).wait()
    swap.wait_send()
    pltpu.make_async_copy(rcv2.at[others], rcv2.at[others], s3).wait()
    most = pl.ds(0, (PLANES - 1) * rows)
    pltpu.make_async_copy(gath.at[most], gath.at[most], r4).wait()
    out_ref[...] = gath[...]
    pltpu.make_async_copy(gath.at[most], gath.at[most], s4).wait()


def fused(*arrays):
    window = arrays[3].shape[1]
    depth = arrays[6].shape[0]
    bf16, f32 = jnp.bfloat16, jnp.float32
    dma = pltpu.SemaphoreType.DMA
    out = pl.pallas_call(
        kernel,
        out_shape=jax.ShapeDtypeStruct((D // QB, QB), bf16),
        in_specs=[pl.BlockSpec(memory_space=pl.ANY)] * 9,
        out_specs=pl.BlockSpec(memory_space=pltpu.VMEM),
        scratch_shapes=[
            pltpu.VMEM((1, HEADS * HD), bf16),
            pltpu.VMEM((1, KVH * HD), bf16),
            pltpu.VMEM((1, KVH * HD), bf16),
            pltpu.VMEM((window, KVH * HD), bf16),
            pltpu.VMEM((window, KVH * HD), bf16),
            pltpu.SMEM((1,), jnp.int32),
            pltpu.SMEM((1, D // QB), f32),
            pltpu.SMEM((1, D // QB), f32),
            pltpu.VMEM((PLANES * PIECES, depth, PIECE), bf16),
            pltpu.VMEM((HEADS, HD), f32),
            pltpu.VMEM((SHARDS, 2 * GROUP, HD), bf16),
            pltpu.VMEM((SHARDS, 2 * GROUP, HD), bf16),
            pltpu.VMEM((PAIR * GROUP, HD), f32),
            pltpu.VMEM((PAIR, BLOCKS, QB), f32),
            pltpu.VMEM((PLANES * PAIR, BLOCKS, QB), bf16),
            pltpu.VMEM((SHARDS * PAIR, BLOCKS, QB), bf16),
            pltpu.VMEM((2, PAIR * BLOCKS, QB), f32),
            pltpu.VMEM((D // QB, QB), bf16),
            dma((8,)), dma((PLANES * PIECES,)),
            dma, dma, dma, dma, dma, dma, dma, dma,
        ],
        compiler_params=pltpu.CompilerParams(
            collective_id=0, has_side_effects=True, vmem_limit_bytes=64 * 1024 * 1024
        ),
    )(*arrays)
    return out.reshape(1, D)


def body_for(mesh):
    sizes = dict(mesh.shape)
    if sizes["tensor"] == KVH and sizes["replica"] == 2 and sizes["dp"] == 2:
        return fused
    return shards


def solution(mesh):
    return jax.shard_map(
        body_for(mesh),
        mesh=mesh,
        in_specs=(
            P(("replica", "dp"), None),
            P(("replica", "dp"), None),
            P(("replica", "dp"), None),
            P(("replica", "dp"), "tensor", None),
            P(("replica", "dp"), "tensor", None),
            P(("replica", "dp")),
            P("tensor", None),
            P(("replica", "dp"), None),
            P(("replica", "dp"), None),
        ),
        out_specs=P(("replica", "dp"), None),
        check_vma=False,
    )
```

```python
import math

import jax
import jax.numpy as jnp
from jax import lax
from jax.experimental import pallas as pl
from jax.experimental.pallas import tpu as pltpu
from jax.sharding import PartitionSpec as P

D = 16384
HEADS = 128
KVH = 8
HD = 128
QB = 128


def shards(
    queries,
    new_keys,
    new_values,
    key_cache,
    value_cache,
    cache_lengths,
    out_weight,
    partial_scales,
    sum_scales,
):
    shard_index = lax.axis_index("tensor")
    shard_count = lax.axis_size("tensor")
    row_count = queries.shape[0]
    window = key_cache.shape[1]
    group_size = HEADS // KVH
    heads_here = HEADS // shard_count
    inv_root = 1.0 / math.sqrt(HD)
    query_heads = queries.reshape(row_count, KVH, group_size, HD)
    keys_local = key_cache.reshape(row_count, window, KVH, HD)
    values_local = value_cache.reshape(row_count, window, KVH, HD)
    scores = (
        jnp.einsum("rkgd,rckd->rkgc", query_heads, keys_local, preferred_element_type=jnp.float32)
        * inv_root
    )
    positions = shard_index * window + jnp.arange(window, dtype=jnp.int32)
    live_mask = (positions[None, :] < cache_lengths[:, None])[:, None, None, :]
    masked = jnp.where(live_mask, scores, -1e30)
    local_top = jnp.max(masked, axis=-1)
    weights = jnp.where(live_mask, jnp.exp(masked - local_top[..., None]), 0.0).astype(jnp.bfloat16)
    local_mass = jnp.sum(weights.astype(jnp.float32), axis=-1)
    local_numer = jnp.einsum(
        "rkgc,rckd->rkgd", weights, values_local, preferred_element_type=jnp.float32
    )
    top_parts = local_top.reshape(row_count, HEADS)
    mass_parts = local_mass.reshape(row_count, HEADS)
    numer_parts = local_numer.reshape(row_count, HEADS, HD)
    first_head = shard_index * heads_here
    start_state = (
        jnp.full((row_count, heads_here), -1e30, jnp.float32),
        jnp.zeros((row_count, heads_here), jnp.float32),
        jnp.zeros((row_count, heads_here, HD), jnp.float32),
    )
    piece_top = lax.dynamic_slice_in_dim(
        lax.all_gather(top_parts[None].astype(jnp.bfloat16), "tensor", axis=0, tiled=True).astype(
            jnp.float32
        ),
        first_head,
        heads_here,
        2,
    )
    piece_mass = lax.dynamic_slice_in_dim(
        lax.all_gather(mass_parts[None].astype(jnp.bfloat16), "tensor", axis=0, tiled=True).astype(
            jnp.float32
        ),
        first_head,
        heads_here,
        2,
    )
    piece_numer = lax.dynamic_slice_in_dim(
        lax.all_gather(numer_parts[None].astype(jnp.bfloat16), "tensor", axis=0, tiled=True).astype(
            jnp.float32
        ),
        first_head,
        heads_here,
        2,
    )
    joined_top = jnp.maximum(start_state[0], jnp.max(piece_top, axis=0))
    piece_factor = jnp.exp(piece_top - joined_top)
    carry_factor = jnp.exp(start_state[0] - joined_top)
    joined_mass = start_state[1] * carry_factor + jnp.sum(piece_mass * piece_factor, axis=0)
    joined_numer = start_state[2] * carry_factor[..., None] + jnp.sum(
        piece_numer * piece_factor[..., None], axis=0
    )
    own_query = lax.dynamic_slice_in_dim(queries, first_head * HD, heads_here * HD, 1).reshape(
        row_count, heads_here, HD
    )
    kv_index = (first_head + jnp.arange(heads_here, dtype=jnp.int32)) // group_size
    picker = (kv_index[:, None] == jnp.arange(KVH, dtype=jnp.int32)[None, :]).astype(jnp.float32)
    own_key = jnp.einsum(
        "hk,rkd->rhd",
        picker,
        new_keys.reshape(row_count, KVH, HD).astype(jnp.float32),
        precision=lax.Precision.HIGHEST,
    )
    own_value = jnp.einsum(
        "hk,rkd->rhd",
        picker,
        new_values.reshape(row_count, KVH, HD).astype(jnp.float32),
        precision=lax.Precision.HIGHEST,
    )
    fresh_score = jnp.sum(own_query.astype(jnp.float32) * own_key, axis=-1) * inv_root
    best_score = jnp.maximum(joined_top, fresh_score)
    old_factor = jnp.exp(joined_top - best_score)
    new_factor = jnp.exp(fresh_score - best_score)
    attended = (joined_numer * old_factor[..., None] + new_factor[..., None] * own_value) / (
        joined_mass * old_factor + new_factor
    )[..., None]
    attended = attended.astype(jnp.bfloat16).reshape(row_count, heads_here * HD)
    partial_value = jnp.dot(attended, out_weight, preferred_element_type=jnp.float32)
    block_count = D // QB
    coded_narrow = jnp.clip(
        partial_value.reshape(row_count, block_count, QB) / partial_scales[..., None], -448.0, 448.0
    ).astype(jnp.bfloat16)
    coded_narrow = lax.optimization_barrier(coded_narrow).reshape(row_count, D)
    summed = lax.psum(coded_narrow.astype(jnp.float32), "tensor")
    reduced = summed.reshape(row_count, block_count, QB) * partial_scales[..., None]
    recoded = jnp.clip(reduced / sum_scales[..., None], -448.0, 448.0).astype(jnp.bfloat16)
    gathered = recoded.reshape(row_count, D)
    result = (
        gathered.reshape(row_count, block_count, QB).astype(jnp.float32) * sum_scales[..., None]
    )
    return result.reshape(row_count, D).astype(jnp.bfloat16)


MESH = pl.DeviceIdType.MESH
PAIR = 2
GROUP = HEADS // KVH
SHARDS = KVH
PLANES = 4
HALF = D // PLANES // PAIR
PIECES = 2
PIECE = HALF // PIECES
BLOCKS = HALF // QB


def flipped(index, k):
    total = 0
    for bit in (1, 2, 4):
        a = (index // bit) % 2
        b = (k // bit) % 2
        total = total + bit * (a + b - 2 * a * b)
    return total


def kernel(
    q_hbm, nk_hbm, nv_hbm, k_hbm, v_hbm, len_hbm, w_hbm, ps_hbm, ss_hbm,
    out_ref,
    q_raw, nk, nv, keys, values, lens, first, second, wbuf, q_rows,
    snd1, rcv1, att, stage, snd2, rcv2, scales, gath,
    in_sem, w_sem, s1, r1, s2, r2, s3, r3, s4, r4,
):
    rep, me, dp = lax.axis_index("replica"), lax.axis_index("tensor"), lax.axis_index("dp")
    plane, side = me // 2, me % 2
    window = keys.shape[0]
    inv_root = 1.0 / math.sqrt(HD)

    def device(shard, core):
        return {"replica": rep, "tensor": shard, "dp": core}

    small = [
        pltpu.make_async_copy(a, b, in_sem.at[i])
        for i, (a, b) in enumerate(
            [
                (q_hbm, q_raw), (k_hbm.at[0], keys), (len_hbm, lens), (v_hbm.at[0], values),
                (nk_hbm, nk), (nv_hbm, nv), (ps_hbm, first), (ss_hbm, second),
            ]
        )
    ]

    def weight_copy(i, p):
        target = flipped(plane, PLANES - 1 - i)
        start = pl.multiple_of(target * (PAIR * HALF) + dp * HALF + p * PIECE, PIECE)
        slot = i * PIECES + p
        return pltpu.make_async_copy(w_hbm.at[:, pl.ds(start, PIECE)], wbuf.at[slot], w_sem.at[slot])

    barrier = pltpu.get_barrier_semaphore()
    for k in range(SHARDS - 1, -1, -1):
        for c in range(PAIR):
            if k or c:
                pl.semaphore_signal(
                    barrier, inc=1, device_id=device(flipped(me, k), (dp + c) % 2), device_id_type=MESH
                )
    for copy in small:
        copy.start()
    for n in range(0, 3):
        weight_copy(n // PIECES, n % PIECES).start()
    for copy in small:
        copy.wait()

    for h in range(HEADS):
        q_rows[h : h + 1, :] = q_raw[0:1, h * HD : (h + 1) * HD].astype(jnp.float32)

    length = lens[0]
    live = (me * window + lax.broadcasted_iota(jnp.int32, (GROUP, window), 1)) < length
    lane = lax.broadcasted_iota(jnp.int32, (GROUP, HD), 1)
    for k in range(KVH):
        query = q_rows[k * GROUP : (k + 1) * GROUP, :].astype(jnp.bfloat16)
        score = (
            lax.dot_general(
                query, keys[:, k * HD : (k + 1) * HD], (((1,), (1,)), ((), ())),
                preferred_element_type=jnp.float32,
            )
            * inv_root
        )
        score = jnp.where(live, score, -1e30)
        top = jnp.max(score, axis=-1, keepdims=True).astype(jnp.bfloat16).astype(jnp.float32)
        weight = jnp.where(live, jnp.exp(score - top), 0.0).astype(jnp.bfloat16)
        mass = jnp.sum(weight.astype(jnp.float32), axis=-1, keepdims=True)
        numer = jnp.dot(weight, values[:, k * HD : (k + 1) * HD], preferred_element_type=jnp.float32)
        coarse = mass.astype(jnp.bfloat16).astype(jnp.float32)
        stats = jnp.where(lane == 0, top, jnp.where(lane == 1, coarse, mass - coarse))
        snd1[k, 0:GROUP, :] = numer.astype(jnp.bfloat16)
        snd1[k, GROUP : 2 * GROUP, :] = stats.astype(jnp.bfloat16)

    for i in range(PAIR * BLOCKS):
        at = plane * (PAIR * BLOCKS) + i
        scales[0, i : i + 1, :] = jnp.full((1, QB), first[0, at], jnp.float32)
        scales[1, i : i + 1, :] = jnp.full((1, QB), second[0, at], jnp.float32)
    own_query = q_rows[pl.ds(pl.multiple_of(me * GROUP, GROUP), GROUP), :]
    own = pl.ds(pl.multiple_of(me * HD, HD), HD)
    own_key = nk[:, own].astype(jnp.float32)
    own_value = nv[:, own].astype(jnp.float32)
    fresh = jnp.sum(own_query * own_key, axis=-1, keepdims=True) * inv_root

    pl.semaphore_wait(barrier, SHARDS * PAIR - 1)

    for k in range(SHARDS - 1, 0, -1):
        shard = flipped(me, k)
        pltpu.make_async_remote_copy(
            snd1.at[shard], rcv1.at[me], s1, r1, device_id=device(shard, dp), device_id_type=MESH
        ).start()
    for n in range(3, 8):
        weight_copy(n // PIECES, n % PIECES).start()
    rcv1[me] = snd1[me]
    pltpu.make_async_copy(rcv1.at[pl.ds(0, SHARDS - 1)], rcv1.at[pl.ds(0, SHARDS - 1)], r1).wait()

    got = [rcv1[t].astype(jnp.float32) for t in range(SHARDS)]
    tops = [g[GROUP:, 0:1] for g in got]
    best = fresh
    for top in tops:
        best = jnp.maximum(best, top)
    fresh_factor = jnp.exp(fresh - best)
    mass = fresh_factor
    numer = fresh_factor * own_value
    for g, top in zip(got, tops):
        factor = jnp.exp(top - best)
        mass = mass + factor * (g[GROUP:, 1:2] + g[GROUP:, 2:3])
        numer = numer + factor * g[:GROUP]
    mine = pl.ds(pl.multiple_of(dp * GROUP, GROUP), GROUP)
    att[mine, :] = (numer / mass).astype(jnp.bfloat16).astype(jnp.float32)

    swap = pltpu.make_async_remote_copy(
        att.at[mine], att.at[mine], s2, r2, device_id=device(me, 1 - dp), device_id_type=MESH
    )
    swap.start()
    swap.wait_recv()
    x = jnp.concatenate(
        [att[pl.ds(h, PAIR, stride=GROUP), :] for h in range(GROUP)], axis=1
    ).astype(jnp.bfloat16)

    def product(i):
        for p in range(PIECES):
            weight_copy(i, p).wait()
            y = jnp.dot(x, wbuf[i * PIECES + p], preferred_element_type=jnp.float32)
            for b in range(PIECE // QB):
                at = p * (PIECE // QB) + b
                for r in range(PAIR):
                    stage[r, at : at + 1, :] = y[r : r + 1, b * QB : (b + 1) * QB]
        for r in range(PAIR):
            snd2[i * PAIR + r] = stage[r].astype(jnp.bfloat16)

    slot = me * PAIR + dp

    def send(i, r, shard):
        pltpu.make_async_remote_copy(
            snd2.at[i * PAIR + r], rcv2.at[slot], s3, r3,
            device_id=device(shard, r), device_id_type=MESH,
        ).start()

    def step(i, carry):
        product(i)
        target = flipped(plane, PLANES - 1 - i)
        for r in range(PAIR):
            send(i, r, target * 2 + 1 - side)
            send(i, r, target * 2 + side)
        return carry

    lax.fori_loop(0, PLANES - 1, step, 0)
    last = PLANES - 1
    product(last)
    send(last, 0, plane * 2 + 1 - side)
    send(last, 1, plane * 2 + 1 - side)
    send(last, 1 - dp, me)
    rcv2[slot] = snd2[last * PAIR + dp]
    others = pl.ds(0, SHARDS * PAIR - 1)
    pltpu.make_async_copy(rcv2.at[others], rcv2.at[others], r3).wait()

    rows = PAIR * BLOCKS
    for h in range(PAIR):
        part = slice(h * BLOCKS, (h + 1) * BLOCKS)
        first_scale, second_scale = scales[0, part, :], scales[1, part, :]
        total = jnp.zeros((BLOCKS, QB), jnp.float32)
        for t in range(SHARDS):
            coded = jnp.clip(rcv2[t * PAIR + h].astype(jnp.float32) / first_scale, -448.0, 448.0)
            total = total + coded.astype(jnp.bfloat16).astype(jnp.float32)
        recoded = jnp.clip(total * first_scale / second_scale, -448.0, 448.0).astype(jnp.bfloat16)
        at = pl.ds(pl.multiple_of(plane * rows + h * BLOCKS, BLOCKS), BLOCKS)
        gath[at, :] = (recoded.astype(jnp.float32) * second_scale).astype(jnp.bfloat16)

    own_rows = pl.ds(pl.multiple_of(plane * rows, rows), rows)
    for k in range(PLANES - 1, 0, -1):
        pltpu.make_async_remote_copy(
            gath.at[own_rows], gath.at[own_rows], s4, r4,
            device_id=device(flipped(plane, k) * 2 + side, dp), device_id_type=MESH,
        ).start()
    pltpu.make_async_copy(snd1.at[pl.ds(0, SHARDS - 1)], snd1.at[pl.ds(0, SHARDS - 1)], s1).wait()
    swap.wait_send()
    pltpu.make_async_copy(rcv2.at[others], rcv2.at[others], s3).wait()
    most = pl.ds(0, (PLANES - 1) * rows)
    pltpu.make_async_copy(gath.at[most], gath.at[most], r4).wait()
    out_ref[...] = gath[...]
    pltpu.make_async_copy(gath.at[most], gath.at[most], s4).wait()


def fused(*arrays):
    window = arrays[3].shape[1]
    depth = arrays[6].shape[0]
    bf16, f32 = jnp.bfloat16, jnp.float32
    dma = pltpu.SemaphoreType.DMA
    out = pl.pallas_call(
        kernel,
        out_shape=jax.ShapeDtypeStruct((D // QB, QB), bf16),
        in_specs=[pl.BlockSpec(memory_space=pl.ANY)] * 9,
        out_specs=pl.BlockSpec(memory_space=pltpu.VMEM),
        scratch_shapes=[
            pltpu.VMEM((1, HEADS * HD), bf16),
            pltpu.VMEM((1, KVH * HD), bf16),
            pltpu.VMEM((1, KVH * HD), bf16),
            pltpu.VMEM((window, KVH * HD), bf16),
            pltpu.VMEM((window, KVH * HD), bf16),
            pltpu.SMEM((1,), jnp.int32),
            pltpu.SMEM((1, D // QB), f32),
            pltpu.SMEM((1, D // QB), f32),
            pltpu.VMEM((PLANES * PIECES, depth, PIECE), bf16),
            pltpu.VMEM((HEADS, HD), f32),
            pltpu.VMEM((SHARDS, 2 * GROUP, HD), bf16),
            pltpu.VMEM((SHARDS, 2 * GROUP, HD), bf16),
            pltpu.VMEM((PAIR * GROUP, HD), f32),
            pltpu.VMEM((PAIR, BLOCKS, QB), f32),
            pltpu.VMEM((PLANES * PAIR, BLOCKS, QB), bf16),
            pltpu.VMEM((SHARDS * PAIR, BLOCKS, QB), bf16),
            pltpu.VMEM((2, PAIR * BLOCKS, QB), f32),
            pltpu.VMEM((D // QB, QB), bf16),
            dma((8,)), dma((PLANES * PIECES,)),
            dma, dma, dma, dma, dma, dma, dma, dma,
        ],
        compiler_params=pltpu.CompilerParams(
            collective_id=0, has_side_effects=True, vmem_limit_bytes=64 * 1024 * 1024
        ),
    )(*arrays)
    return out.reshape(1, D)


def body_for(mesh):
    sizes = dict(mesh.shape)
    if sizes["tensor"] == KVH and sizes["replica"] == 2 and sizes["dp"] == 2:
        return fused
    return shards


def solution(mesh):
    return jax.shard_map(
        body_for(mesh),
        mesh=mesh,
        in_specs=(
            P(("replica", "dp"), None),
            P(("replica", "dp"), None),
            P(("replica", "dp"), None),
            P(("replica", "dp"), "tensor", None),
            P(("replica", "dp"), "tensor", None),
            P(("replica", "dp")),
            P("tensor", None),
            P(("replica", "dp"), None),
            P(("replica", "dp"), None),
        ),
        out_specs=P(("replica", "dp"), None),
        check_vma=False,
    )
```
